32 devices in a mesh: group: 2 (over x), blk: 16 (over z, y, core).
Axes of the slice: x: 2, y: 2, z: 4, core: 2. Of those that a mesh axis runs over, the one named last changes fastest.
Arguments:
- queries: bfloat16 [4096, 512], P(('group', 'blk')), parts along dimension 0, may hold values from -8 to 8
- keys: bfloat16 [4096, 512], P(('group', 'blk')), parts along dimension 0, may hold values from -8 to 8
- values: bfloat16 [4096, 512], P(('group', 'blk')), parts along dimension 0, may hold values from -6 to 6
- outputs: bfloat16 [4096, 512], P(('group', 'blk')), parts along dimension 0, may hold values from -6 to 6
- grad_out: bfloat16 [4096, 512], P(('group', 'blk')), parts along dimension 0, may hold values from -16 to 16
- block_mask: int32 [32, 16], P(('group', 'blk')), parts along dimension 0, may hold values from 0 to 1, as said below
- neighbours: int32 [4096, 6], P(('group', 'blk')), parts along dimension 0, may hold values from -1 to 2047, as said below
- conv_weight: float32 [6, 512], replicated, may hold values from -0.125 to 0.125
Outputs:
- grad_queries: bfloat16 [4096, 512], P(('group', 'blk')), parts along dimension 0
- grad_keys: bfloat16 [4096, 512], P(('group', 'blk')), parts along dimension 0
- grad_values: bfloat16 [4096, 512], P(('group', 'blk')), parts along dimension 0
The draws below stay inside these ranges and needn't reach their ends.
There are 2 independent parts, one for each index of `group`. The reference program is written for one: setup_inputs(seed, part) draws one part's arguments, and reference() takes and returns one part's arrays. A program takes and returns all parts, laid end to end along the dimension named above; an argument that names none is the same for every part. Nothing has to cross between parts.
Inputs may be any that keep to these rules, and one draw needn't show every extreme that they name: Every diagonal entry is 1; block_mask[a, b] = 1 where the 128 queries of block a (one index of blk) attend to the keys of block b. `neighbours`: each entry is -1 or a token index that differs from its row's own index by at most 128; the difference 128 occurs.
All inputs are finite; a program needn't handle non-finite values.
Results may differ from the reference program's by a relative error of at most 0.0052.
Values may be sent and summed in bfloat16 or wider, within the bound.
A program may use at most 128 MiB of HBM per device.

```python
import jax
import jax.numpy as jnp
from jax import lax

HEADS = 8
HD = 64
CH = 512
TOK_DEV = 128
FACES = 6
BLOCKS = 16
TOKENS = 2048


def drawn_rows(key, which):
    channels = HEADS * HD
    base = jnp.clip(jax.random.normal(jax.random.fold_in(key, 11 + which), (TOKENS, channels), jnp.float32), -4.0, 4.0)
    return base.astype(jnp.bfloat16)


def draw_queries(key, part):
    return drawn_rows(key, 0)


def draw_keys(key, part):
    return drawn_rows(key, 1)


def draw_block_mask(key, part):
    level = jax.random.randint(jax.random.fold_in(key, 31), (BLOCKS,), 0, 4)
    thresholds = jnp.array([64, 32, 16, 8], jnp.int32)[level]
    draws_int = jax.random.randint(jax.random.fold_in(key, 32), (BLOCKS, BLOCKS), 0, 64)
    bits = draws_int < thresholds[:, None]
    diagonal = jnp.arange(BLOCKS)[:, None] == jnp.arange(BLOCKS)[None, :]
    return jnp.where(bits | diagonal, 1, 0).astype(jnp.int32)


def draw_neighbours(key, part):
    offsets = jax.random.randint(jax.random.fold_in(key, 41), (TOKENS, FACES), -TOK_DEV, TOK_DEV + 1)
    present = jax.random.randint(jax.random.fold_in(key, 42), (TOKENS, FACES), 0, 4) > 0
    target = jnp.arange(TOKENS, dtype=jnp.int32)[:, None] + offsets
    result = jnp.where(present & (target >= 0) & (target < TOKENS), target, -1)
    result = result.at[TOKENS - 1 - TOK_DEV, 0].set(TOKENS - 1)
    result = result.at[0, 1].set(-1)
    return result.astype(jnp.int32)


def level_of(own_key, dims, pieces, least, largest):
    gain = 1.0
    for axis_at, blocks in pieces:
        draws = jax.random.uniform(jax.random.fold_in(jax.random.fold_in(own_key, 6), axis_at), (blocks,), jnp.float32, least / len(pieces), largest / len(pieces))
        gain = gain * jnp.repeat(jnp.exp(draws), dims[axis_at] // blocks).reshape((-1,) + (1,) * (len(dims) - 1 - axis_at))
    return gain


def scatter_about(own_key, shape, deviation, most, cuts=(), kind=jnp.bfloat16):
    factor_of = level_of(own_key, shape, cuts, -0.22, 0.18) if cuts else 1.0
    values = jax.random.normal(own_key, shape, jnp.float32) * deviation * factor_of
    return jnp.minimum(jnp.maximum(values, -most), most).astype(kind)


def setup_inputs(seed: int = 0, part: int = 0) -> dict:
    splits = jax.random.split(jax.random.key(seed), 9)
    part_splits = jax.random.split(jax.random.fold_in(splits[8], part), 9)
    return {
        "queries": draw_queries(jax.random.fold_in(jax.random.fold_in(splits[8], part), 71), part),
        "keys": draw_keys(jax.random.fold_in(jax.random.fold_in(splits[8], part), 71), part),
        "values": scatter_about(part_splits[2], (TOKENS, CH), 1.0, 6.0, ((0, 16),)),
        "outputs": scatter_about(part_splits[3], (TOKENS, CH), 1.0, 6.0, ((0, 16),)),
        "grad_out": jnp.clip(jax.random.uniform(part_splits[4], (TOKENS, CH), jnp.float32, -16.0, 16.0) * level_of(part_splits[4], (TOKENS, CH), ((0, 16),), -0.4, 0.0), -16.0, 16.0).astype(jnp.bfloat16),
        "block_mask": draw_block_mask(jax.random.fold_in(jax.random.fold_in(splits[8], part), 71), part),
        "neighbours": draw_neighbours(jax.random.fold_in(jax.random.fold_in(splits[8], part), 71), part),
        "conv_weight": scatter_about(splits[7], (FACES, CH), (400 * FACES) ** -0.5, 0.125, (), jnp.float32),
    }


def reference(queries, keys, values, outputs, grad_out, block_mask, neighbours, conv_weight):
    token_count = queries.shape[0]
    channels = queries.shape[1]
    row_count = TOK_DEV
    block_total = token_count // row_count
    score_scale = HD ** -0.5
    highest = lax.Precision.HIGHEST
    query_all = queries.astype(jnp.float32).reshape(token_count, HEADS, HD)
    key_all = keys.astype(jnp.float32).reshape(token_count, HEADS, HD)
    value_all = values.astype(jnp.float32).reshape(token_count, HEADS, HD)
    grad_all = grad_out.astype(jnp.float32).reshape(token_count, HEADS, HD)
    output_all = outputs.astype(jnp.float32).reshape(token_count, HEADS, HD)
    row_delta = jnp.sum(grad_all * output_all, axis=2)
    key_owner = (jnp.arange(token_count) // row_count).astype(jnp.int32)

    def one_block(running, number):
        grad_key_sum, grad_value_sum = running
        begin_row = (number * row_count).astype(jnp.int32)
        query_block = lax.dynamic_slice_in_dim(query_all, begin_row, row_count, 0)
        grad_block = lax.dynamic_slice_in_dim(grad_all, begin_row, row_count, 0)
        delta_block = lax.dynamic_slice_in_dim(row_delta, begin_row, row_count, 0)
        mask_line = lax.dynamic_index_in_dim(block_mask, number, 0, keepdims=False)
        live_cols = mask_line[key_owner] > 0
        scores = score_scale * jnp.einsum("thd,shd->ths", query_block, key_all, precision=highest)
        scores = jnp.where(live_cols[None, None, :], scores, -jnp.inf)
        log_total = jax.nn.logsumexp(scores, axis=2)
        weights = jnp.exp(scores - log_total[:, :, None])
        grad_prob = jnp.einsum("thd,shd->ths", grad_block, value_all, precision=highest)
        grad_score = weights * (grad_prob - delta_block[:, :, None])
        grad_query = score_scale * jnp.einsum("ths,shd->thd", grad_score, key_all, precision=highest)
        weights_low = lax.optimization_barrier(weights.astype(jnp.bfloat16)).astype(jnp.float32)
        score_low = lax.optimization_barrier(grad_score.astype(jnp.bfloat16)).astype(jnp.float32)
        grad_value_sum = grad_value_sum + jnp.einsum("ths,thd->shd", weights_low, grad_block, precision=highest)
        grad_key_sum = grad_key_sum + score_scale * jnp.einsum("ths,thd->shd", score_low, query_block, precision=highest)
        return (grad_key_sum, grad_value_sum), grad_query.astype(jnp.bfloat16)

    empty = jnp.zeros((token_count, HEADS, HD), jnp.float32)
    sums, query_parts = lax.scan(one_block, (empty, empty), jnp.arange(block_total, dtype=jnp.int32))
    grad_key_sum, grad_value_sum = sums
    grad_queries = query_parts.reshape(token_count, channels)
    usable = neighbours >= 0
    targets = jnp.where(usable, neighbours, 0).astype(jnp.int32)
    contributions = jnp.where(usable[:, :, None], conv_weight.astype(jnp.float32)[None, :, :] * grad_out.astype(jnp.float32)[:, None, :], 0.0)
    conv_grad = jnp.zeros((token_count, channels), jnp.float32).at[targets.reshape(-1)].add(contributions.reshape(-1, channels))
    grad_keys = grad_key_sum.reshape(token_count, channels).astype(jnp.bfloat16)
    grad_values = (grad_value_sum.reshape(token_count, channels) + conv_grad).astype(jnp.bfloat16)
    return grad_queries, grad_keys, grad_values
```

```python
import functools

import jax
import jax.numpy as jnp
from jax import lax
from jax.experimental import pallas as pl
from jax.experimental.pallas import tpu as pltpu
from jax.sharding import PartitionSpec as P

HEADS = 8
HD = 64
LANES = 128
F32 = jnp.float32
BF16 = jnp.bfloat16
NEG_LARGE = -1e30
NT = (((1,), (1,)), ((), ()))


def kernel(
    n,
    q_ref,
    k_ref,
    v_ref,
    o_ref,
    g_ref,
    mask_ref,
    nb_ref,
    cw_ref,
    dq_ref,
    dk_ref,
    dv_ref,
    kvs,
    qgs,
    sms,
    kv,
    qg,
    sm,
    kvt,
    w,
    bias,
    sbuf,
    dbuf,
    dsp,
    cvs,
    cvr,
    cvo,
    dqs,
    dqr,
    rds,
    rdr,
    outs,
    outr,
    kv_ss,
    kv_rs,
    qg_ss,
    qg_rs,
    sm_ss,
    sm_rs,
    fw_ss,
    fw_rs,
    cv_ss,
    cv_rs,
    dq_ss,
    dq_rs,
    rd_ss,
    rd_rs,
    out_ss,
    out_rs,
    lc_s,
):
    parts = n // HEADS
    rows = q_ref.shape[0]
    faces = nb_ref.shape[1]
    scale = HD**-0.5
    me = lax.axis_index("blk")
    head = me // parts
    part = me % parts

    def peer(d):
        return lax.rem(head + d, HEADS)

    def sibling(e):
        return lax.rem(part + e, parts)

    def at(index):
        return {"blk": index}

    above, below = lax.rem(me + n - 1, n), lax.rem(me + 1, n)

    barrier = pltpu.get_barrier_semaphore()
    partners = [peer(d) * parts + part for d in range(1, HEADS)]
    partners += [head * parts + sibling(e) for e in range(1, parts)]
    partners += [above, below]
    for other in partners:
        pl.semaphore_signal(barrier, inc=1, device_id=at(other), device_id_type=pl.DeviceIdType.MESH)

    def remote(src, dst, ss, rs, index):
        return pltpu.make_async_remote_copy(
            src_ref=src,
            dst_ref=dst,
            send_sem=ss,
            recv_sem=rs,
            device_id=at(index),
            device_id_type=pl.DeviceIdType.MESH,
        )

    for h in range(HEADS):
        cols = slice(h * HD, (h + 1) * HD)
        kvs[h] = jnp.concatenate([k_ref[:, cols], v_ref[:, cols]], axis=1)
        scaled = (q_ref[:, cols].astype(F32) * scale).astype(BF16)
        qgs[h] = jnp.concatenate([scaled, g_ref[:, cols]], axis=1)
    grads = g_ref[...].astype(F32)
    product = grads * o_ref[...].astype(F32)
    channels = product.shape[1]
    pick = (
        lax.broadcasted_iota(jnp.int32, (HEADS, channels), 1) // HD
        == lax.broadcasted_iota(jnp.int32, (HEADS, channels), 0)
    ).astype(F32)
    delta = lax.dot_general(
        pick, product, NT, precision=lax.Precision.HIGHEST, preferred_element_type=F32
    )
    mask_row = jnp.concatenate(
        [mask_ref[...].astype(F32), jnp.zeros((1, LANES - n), F32)], axis=1
    )
    sms[...] = jnp.zeros_like(sms)
    for h in range(HEADS):
        sms[h, 0:1, :] = delta[h : h + 1, :]
        sms[h, 1:2, :] = mask_row

    pl.semaphore_wait(barrier, len(partners))

    own = [
        pltpu.make_async_copy(kvs.at[head], kv.at[me], lc_s.at[0]),
        pltpu.make_async_copy(qgs.at[head], qg.at[head], lc_s.at[1]),
        pltpu.make_async_copy(sms.at[head], sm.at[head], lc_s.at[2]),
    ]
    kv_copies, qg_copies, sm_copies = [], [], []
    for d in range(1, HEADS):
        to, at_to = peer(d), peer(d) * parts + part
        kv_copies.append(
            remote(kvs.at[to], kv.at[me], kv_ss.at[d - 1], kv_rs.at[d - 1], at_to)
        )
        qg_copies.append(
            remote(qgs.at[to], qg.at[head], qg_ss.at[d - 1], qg_rs.at[d - 1], at_to)
        )
        sm_copies.append(
            remote(sms.at[to], sm.at[head], sm_ss.at[d - 1], sm_rs.at[d - 1], at_to)
        )
    for copy in own + kv_copies + qg_copies + sm_copies:
        copy.start()

    wide_nb = jnp.concatenate(
        [nb_ref[...].astype(F32), jnp.zeros((rows, LANES - faces), F32)], axis=1
    )
    turned = wide_nb.T.astype(jnp.int32)
    hits, terms = [], []
    for f in range(faces):
        line = turned[f : f + 1, :]
        where_to = jnp.where(line >= 0, line - me * rows + rows, -1)
        slots = lax.broadcasted_iota(jnp.int32, (3 * rows, rows), 0)
        hits.append((slots == where_to).astype(F32).astype(BF16))
        terms.append(grads * cw_ref[f : f + 1, :])
    hit = jnp.concatenate(hits, axis=1)
    term = jnp.concatenate(terms, axis=0)
    high = term.astype(BF16)
    low = (term - high.astype(F32)).astype(BF16)
    for b in range(3):
        block = hit[b * rows : (b + 1) * rows]
        spread = jnp.dot(block, high, preferred_element_type=F32) + jnp.dot(
            block, low, preferred_element_type=F32
        )
        if b == 1:
            cvo[...] = spread
        else:
            cvs[b // 2] = spread.astype(BF16)
    cv_copies = [
        remote(cvs.at[0], cvr.at[0], cv_ss.at[0], cv_rs.at[0], above),
        remote(cvs.at[1], cvr.at[1], cv_ss.at[1], cv_rs.at[1], below),
    ]
    for copy in cv_copies:
        copy.start()

    for copy in own:
        copy.wait()
    forwards = []
    for d in range(HEADS):
        source = lax.rem(head - d + HEADS, HEADS) * parts + part
        if d:
            kv_copies[d - 1].wait_recv()
        for e in range(1, parts):
            copy = remote(
                kv.at[source],
                kv.at[source],
                fw_ss.at[e - 1, d],
                fw_rs.at[e - 1, d],
                head * parts + sibling(e),
            )
            copy.start()
            forwards.append(copy)
    for copy in qg_copies + sm_copies:
        copy.wait_recv()
    first_half = lax.broadcasted_iota(jnp.int32, (rows, LANES), 1) < HD
    for i in range(HEADS):
        tile = qg[i].astype(F32)
        w[i * 2 * rows : i * 2 * rows + rows, :] = jnp.where(first_half, tile, 0.0).astype(BF16)
        w[i * 2 * rows + rows : (i + 1) * 2 * rows, :] = jnp.where(
            first_half, 0.0, tile
        ).astype(BF16)
    for copy in forwards:
        copy.wait_recv()

    def turn(j, carry):
        tile = kv[j].astype(F32).T
        kvt[:, pl.ds(pl.multiple_of(j * rows, rows), rows)] = tile[:HD].astype(BF16)
        return carry

    lax.fori_loop(0, n, turn, 0)

    chunk = 4
    chunks = n // chunk
    eye = lax.broadcasted_iota(jnp.int32, (n, LANES), 0) == lax.broadcasted_iota(
        jnp.int32, (n, LANES), 1
    )

    def dq_copy(t, i):
        return remote(
            dqs.at[t], dqr.at[head], dq_ss.at[t], dq_rs.at[t], i * parts + part
        )

    def queries_of(t, carry):
        i = lax.rem(head + t + 1, HEADS)
        w_i = w[pl.ds(pl.multiple_of(i * 2 * rows, 2 * rows), 2 * rows), :]
        delta_i = sm[i, 0:1, :]
        live = jnp.sum(jnp.where(eye, sm[i, 1:2, :], 0.0), axis=1, keepdims=True)
        bias[...] = jnp.broadcast_to((1.0 - live) * NEG_LARGE, (n, LANES))

        def scores(c, top):
            tile = kv[pl.ds(c * chunk, chunk)].reshape(chunk * rows, LANES)
            both = lax.dot_general(tile, w_i, NT, preferred_element_type=F32)
            for b in range(chunk):
                part_of = both[b * rows : (b + 1) * rows]
                s = part_of[:, :rows] + bias[pl.ds(c * chunk + b, 1), :]
                sbuf[c * chunk + b] = s
                dbuf[c * chunk + b] = part_of[:, rows:] - delta_i
                top = jnp.maximum(top, jnp.max(s.reshape(rows // 8, 8, rows), axis=0))
            return top

        top = lax.fori_loop(0, chunks, scores, jnp.full((8, rows), -jnp.inf, F32))
        top = jnp.max(top, axis=0, keepdims=True)

        def weigh(c, total):
            for b in range(chunk):
                e = jnp.exp(sbuf[c * chunk + b] - top)
                sbuf[c * chunk + b] = e
                total = total + jnp.sum(e.reshape(rows // 8, 8, rows), axis=0)
            return total

        total = lax.fori_loop(0, chunks, weigh, jnp.zeros((8, rows), F32))
        inverse = 1.0 / jnp.sum(total, axis=0, keepdims=True)
        left = pl.multiple_of(i * 2 * rows, 2 * rows)

        def combine(c, carry):
            for b in range(chunk):
                p = sbuf[c * chunk + b] * inverse
                ds = p * dbuf[c * chunk + b]
                dsp[c * chunk + b, :, pl.ds(left, rows)] = ds.astype(BF16)
                dsp[c * chunk + b, :, pl.ds(left + rows, rows)] = p.astype(BF16)
            return carry

        lax.fori_loop(0, chunks, combine, 0)
        ds_all = dsp[:, :, pl.ds(left, rows)].reshape(n * rows, rows)
        dq = jnp.dot(kvt[...], ds_all, preferred_element_type=F32) * scale

        @pl.when(t < HEADS - 1)
        def _():
            dqs[t] = dq.astype(BF16)
            dq_copy(t, i).start()

        @pl.when(t == HEADS - 1)
        def _():
            dqr[head] = dq.astype(BF16)

        return carry

    lax.fori_loop(0, HEADS, queries_of, 0)

    def key_sums(j):
        return jnp.dot(dsp[j], w[...], preferred_element_type=F32)

    def rd_copy(e, t):
        return remote(
            rds.at[e - 1, t],
            rdr.at[e - 1, t],
            rd_ss.at[e - 1, t],
            rd_rs.at[e - 1, t],
            head * parts + sibling(e),
        )

    for e in range(1, parts):

        def for_sibling(t, carry, e=e):
            rds[e - 1, t] = key_sums(t * parts + sibling(e))
            rd_copy(e, t).start()
            return carry

        lax.fori_loop(0, HEADS, for_sibling, 0)

    def out_copy(t, i):
        return remote(
            outs.at[t], outr.at[head], out_ss.at[t], out_rs.at[t], i * parts + part
        )

    def for_owner(t, carry):
        i = lax.rem(head + t + 1, HEADS)
        total = key_sums(i * parts + part)
        for e in range(1, parts):
            rd_copy(e, i).wait_recv()
            total = total + rdr[e - 1, i]

        @pl.when(t < HEADS - 1)
        def _():
            outs[t] = total.astype(BF16)
            out_copy(t, i).start()

        @pl.when(t == HEADS - 1)
        def _():
            outr[head] = total.astype(BF16)

        return carry

    lax.fori_loop(0, HEADS, for_owner, 0)

    for t in range(HEADS - 1):
        dq_copy(t, 0).wait_recv()
    turned_dq = dqr[...].astype(F32).reshape(HEADS * HD, rows).T
    dq_ref[...] = turned_dq.astype(BF16)
    for copy in cv_copies:
        copy.wait_recv()
    conv = cvo[...] + cvr[0].astype(F32) + cvr[1].astype(F32)
    for t in range(HEADS - 1):
        out_copy(t, 0).wait_recv()
    tiles = [outr[h].astype(F32) for h in range(HEADS)]
    dk_ref[...] = jnp.concatenate([tile[:, :HD] for tile in tiles], axis=1).astype(BF16)
    dv_ref[...] = (jnp.concatenate([tile[:, HD:] for tile in tiles], axis=1) + conv).astype(BF16)

    for copy in kv_copies + qg_copies + sm_copies + cv_copies + forwards:
        copy.wait_send()
    for t in range(HEADS - 1):
        dq_copy(t, 0).wait_send()
        out_copy(t, 0).wait_send()
    for e in range(1, parts):
        for t in range(HEADS):
            rd_copy(e, t).wait_send()


def body(queries, keys, values, outputs, grad_out, block_mask, neighbours, conv_weight):
    n = lax.axis_size("blk")
    rows, channels = queries.shape
    parts = n // HEADS
    dma = pltpu.SemaphoreType.DMA
    vmem = pl.BlockSpec(memory_space=pltpu.VMEM)
    shape = jax.ShapeDtypeStruct((rows, channels), BF16)
    others = HEADS - 1
    return pl.pallas_call(
        functools.partial(kernel, n),
        out_shape=(shape, shape, shape),
        in_specs=[vmem] * 8,
        out_specs=(vmem, vmem, vmem),
        scratch_shapes=[
            pltpu.VMEM((HEADS, rows, LANES), BF16),
            pltpu.VMEM((HEADS, rows, LANES), BF16),
            pltpu.VMEM((HEADS, 8, LANES), F32),
            pltpu.VMEM((n, rows, LANES), BF16),
            pltpu.VMEM((HEADS, rows, LANES), BF16),
            pltpu.VMEM((HEADS, 8, LANES), F32),
            pltpu.VMEM((HD, n * rows), BF16),
            pltpu.VMEM((HEADS * 2 * rows, LANES), BF16),
            pltpu.VMEM((n, LANES), F32),
            pltpu.VMEM((n, rows, rows), F32),
            pltpu.VMEM((n, rows, rows), F32),
            pltpu.VMEM((n, rows, HEADS * 2 * rows), BF16),
            pltpu.VMEM((2, rows, channels), BF16),
            pltpu.VMEM((2, rows, channels), BF16),
            pltpu.VMEM((rows, channels), F32),
            pltpu.VMEM((HEADS, HD, rows), BF16),
            pltpu.VMEM((HEADS, HD, rows), BF16),
            pltpu.VMEM((parts - 1, HEADS, rows, LANES), F32),
            pltpu.VMEM((parts - 1, HEADS, rows, LANES), F32),
            pltpu.VMEM((HEADS, rows, LANES), BF16),
            pltpu.VMEM((HEADS, rows, LANES), BF16),
            dma((others,)),
            dma((others,)),
            dma((others,)),
            dma((others,)),
            dma((others,)),
            dma((others,)),
            dma((parts - 1, HEADS)),
            dma((parts - 1, HEADS)),
            dma((2,)),
            dma((2,)),
            dma((others,)),
            dma((others,)),
            dma((parts - 1, HEADS)),
            dma((parts - 1, HEADS)),
            dma((others,)),
            dma((others,)),
            dma((3,)),
        ],
        compiler_params=pltpu.CompilerParams(
            collective_id=0, has_side_effects=True, vmem_limit_bytes=60 * 2**20
        ),
    )(queries, keys, values, outputs, grad_out, block_mask, neighbours, conv_weight)


def solution(mesh):
    tokens = P(("group", "blk"), None)
    return jax.shard_map(
        body,
        mesh=mesh,
        in_specs=(tokens,) * 7 + (P(),),
        out_specs=(tokens,) * 3,
        check_vma=False,
    )
```

```python
import functools

import jax
import jax.numpy as jnp
from jax import lax
from jax.experimental import pallas as pl
from jax.experimental.pallas import tpu as pltpu
from jax.sharding import PartitionSpec as P

HEADS = 8
HD = 64
LANES = 128
F32 = jnp.float32
BF16 = jnp.bfloat16
NEG_LARGE = -1e30
NT = (((1,), (1,)), ((), ()))


def kernel(
    n,
    early,
    q_ref,
    k_ref,
    v_ref,
    o_ref,
    g_ref,
    mask_ref,
    nb_ref,
    cw_ref,
    dq_ref,
    dk_ref,
    dv_ref,
    kvs,
    qgs,
    sms,
    kv,
    qg,
    sm,
    kvt,
    w,
    add,
    tops,
    sbuf,
    dsp,
    dkv,
    cvs,
    cvr,
    cvo,
    dqs,
    dqr,
    rds,
    rdr,
    outs,
    outr,
    kv_ss,
    kv_rs,
    qg_ss,
    qg_rs,
    sm_ss,
    sm_rs,
    fw_ss,
    fw_rs,
    cv_ss,
    cv_rs,
    dq_ss,
    dq_rs,
    rd_ss,
    rd_rs,
    out_ss,
    out_rs,
    lc_s,
):
    parts = n // HEADS
    rows = q_ref.shape[0]
    faces = nb_ref.shape[0]
    scale = HD**-0.5
    me = lax.axis_index("blk")
    head = me // parts
    part = me % parts

    def peer(d):
        return lax.rem(head + d, HEADS)

    def sibling(e):
        return lax.rem(part + e, parts)

    def at(index):
        return {"blk": index}

    above, below = lax.rem(me + n - 1, n), lax.rem(me + 1, n)

    barrier = pltpu.get_barrier_semaphore()
    partners = [peer(d) * parts + part for d in range(1, HEADS)]
    partners += [head * parts + sibling(e) for e in range(1, parts)]
    partners += [above, below]
    for other in partners:
        pl.semaphore_signal(barrier, inc=1, device_id=at(other), device_id_type=pl.DeviceIdType.MESH)

    def remote(src, dst, ss, rs, index):
        return pltpu.make_async_remote_copy(
            src_ref=src,
            dst_ref=dst,
            send_sem=ss,
            recv_sem=rs,
            device_id=at(index),
            device_id_type=pl.DeviceIdType.MESH,
        )

    for h in range(HEADS):
        cols = slice(h * HD, (h + 1) * HD)
        scaled = (q_ref[:, cols].astype(F32) * scale).astype(BF16)
        qgs[h] = jnp.concatenate([scaled, g_ref[:, cols]], axis=1)
    sms[...] = jnp.zeros_like(sms)

    pl.semaphore_wait(barrier, len(partners))

    def exchange(buffer, target, ss, rs):
        copies = [
            remote(buffer.at[peer(d)], target, ss.at[d - 1], rs.at[d - 1], peer(d) * parts + part)
            for d in range(1, HEADS)
        ]
        for copy in copies:
            copy.start()
        return copies

    own = [
        pltpu.make_async_copy(kvs.at[head], kv.at[me], lc_s.at[0]),
        pltpu.make_async_copy(qgs.at[head], qg.at[head], lc_s.at[1]),
        pltpu.make_async_copy(sms.at[head], sm.at[head], lc_s.at[2]),
    ]
    own[1].start()
    qg_copies = exchange(qgs, qg.at[head], qg_ss, qg_rs)
    for h in range(HEADS):
        cols = slice(h * HD, (h + 1) * HD)
        kvs[h] = jnp.concatenate([k_ref[:, cols], v_ref[:, cols]], axis=1)
    own[0].start()
    kv_copies = exchange(kvs, kv.at[me], kv_ss, kv_rs)

    grads = g_ref[...].astype(F32)
    product = grads * o_ref[...].astype(F32)
    channels = product.shape[1]
    pick = (
        lax.broadcasted_iota(jnp.int32, (HEADS, channels), 1) // HD
        == lax.broadcasted_iota(jnp.int32, (HEADS, channels), 0)
    ).astype(F32)
    delta = lax.dot_general(
        pick, product, NT, precision=lax.Precision.HIGHEST, preferred_element_type=F32
    )
    mask_row = jnp.concatenate(
        [mask_ref[...].astype(F32), jnp.zeros((1, LANES - n), F32)], axis=1
    )
    for h in range(HEADS):
        sms[h, 0:1, :] = delta[h : h + 1, :]
        sms[h, 1:2, :] = mask_row
    own[2].start()
    sm_copies = exchange(sms, sm.at[head], sm_ss, sm_rs)

    hits, terms = [], []
    for f in range(faces):
        line = nb_ref[f : f + 1, :]
        where_to = jnp.where(line >= 0, line - me * rows + rows, -1)
        slots = lax.broadcasted_iota(jnp.int32, (3 * rows, rows), 0)
        hits.append((slots == where_to).astype(F32).astype(BF16))
        terms.append(grads * cw_ref[f : f + 1, :])
    hit = jnp.concatenate(hits, axis=1)
    term = jnp.concatenate(terms, axis=0)
    high = term.astype(BF16)
    low = (term - high.astype(F32)).astype(BF16)
    for b in range(3):
        block = hit[b * rows : (b + 1) * rows]
        spread = jnp.dot(block, high, preferred_element_type=F32) + jnp.dot(
            block, low, preferred_element_type=F32
        )
        if b == 1:
            cvo[...] = spread
        else:
            cvs[b // 2] = spread.astype(BF16)
    cv_copies = [
        remote(cvs.at[0], cvr.at[0], cv_ss.at[0], cv_rs.at[0], above),
        remote(cvs.at[1], cvr.at[1], cv_ss.at[1], cv_rs.at[1], below),
    ]
    for copy in cv_copies:
        copy.start()

    pair = 4 * rows
    for copy in own:
        copy.wait()
    for copy in qg_copies + sm_copies:
        copy.wait_recv()
    first_half = lax.broadcasted_iota(jnp.int32, (rows, LANES), 1) < HD
    eye = lax.broadcasted_iota(jnp.int32, (n, LANES), 0) == lax.broadcasted_iota(
        jnp.int32, (n, LANES), 1
    )
    for i in range(HEADS):
        tile = qg[i].astype(F32)
        at_q = i // 2 * pair + i % 2 * rows
        at_g = at_q + 2 * rows
        w[at_q : at_q + rows, :] = jnp.where(first_half, tile, 0.0).astype(BF16)
        w[at_g : at_g + rows, :] = jnp.where(first_half, 0.0, tile).astype(BF16)
        live = jnp.sum(jnp.where(eye, sm[i, 1:2, :], 0.0), axis=1, keepdims=True)
        add[:, at_q : at_q + rows] = jnp.broadcast_to((1.0 - live) * NEG_LARGE, (n, rows))
        add[:, at_g : at_g + rows] = jnp.broadcast_to(-sm[i, 0:1, :], (n, rows))
    tops[...] = jnp.full_like(tops, -jnp.inf)

    def score(js, a, w_a):
        lhs = jnp.concatenate([kv[j] for j in js], axis=0)
        both = lax.dot_general(lhs, w_a, NT, preferred_element_type=F32)
        slot = a if early else 0
        top = tops[a]
        for b, j in enumerate(js):
            tile = both[b * rows : (b + 1) * rows] + add[pl.ds(j, 1), pl.ds(a * pair, pair)]
            sbuf[slot, j] = tile
            s = tile[:, : 2 * rows]
            top = jnp.maximum(top, jnp.max(s.reshape(rows // 8, 8, 2 * rows), axis=0))
        tops[a] = top

    def turn(j):
        tile = kv[j].astype(F32).T
        kvt[:, pl.ds(pl.multiple_of(j * rows, rows), rows)] = tile[:HD].astype(BF16)

    def arrived(js):
        for j in js:
            turn(j)
        if early:
            for a in range(HEADS // 2):
                score(js, a, w[a * pair : (a + 1) * pair, :])

    forwards = []
    waiting = []
    for d in range(HEADS + 1):
        js = []
        ready = waiting
        waiting = []
        if d < HEADS:
            chip = lax.rem(head - d + HEADS, HEADS)
            source = chip * parts + part
            if d:
                kv_copies[d - 1].wait_recv()
            for e in range(1, parts):
                copy = remote(
                    kv.at[source],
                    kv.at[source],
                    fw_ss.at[e - 1, d],
                    fw_rs.at[e - 1, d],
                    head * parts + sibling(e),
                )
                copy.start()
                forwards.append(copy)
                waiting.append((copy, chip * parts + lax.rem(part - e + parts, parts)))
            js.append(source)
        for copy, j in ready:
            copy.wait_recv()
            js.append(j)
        arrived(js)

    chunk = 2
    chunks = n // chunk

    def dq_copy(i, u):
        return remote(dqs.at[i], dqr.at[head], dq_ss.at[i], dq_rs.at[u], i * parts + part)

    def pair_of(t, carry):
        a = lax.rem(head // 2 + t + 1, HEADS // 2)
        at_a = pl.multiple_of(a * pair, pair)
        w_a = w[pl.ds(at_a, pair), :]
        slot = a if early else 0
        left = at_a if early else 0
        if not early:

            def scores(c, carry):
                score([c * chunk + b for b in range(chunk)], a, w_a)
                return carry

            lax.fori_loop(0, chunks, scores, 0)
        top = jnp.max(tops[a], axis=0, keepdims=True)

        def weigh(c, total):
            for b in range(chunk):
                e = jnp.exp(sbuf[slot, c * chunk + b, :, : 2 * rows] - top)
                sbuf[slot, c * chunk + b, :, : 2 * rows] = e
                total = total + jnp.sum(e.reshape(rows // 8, 8, 2 * rows), axis=0)
            return total

        total = lax.fori_loop(0, chunks, weigh, jnp.zeros((8, 2 * rows), F32))
        inverse = 1.0 / jnp.sum(total, axis=0, keepdims=True)

        def combine(c, carry):
            for b in range(chunk):
                j = c * chunk + b
                p = sbuf[slot, j, :, : 2 * rows] * inverse
                ds = p * sbuf[slot, j, :, 2 * rows :]
                dsp[j, :, pl.ds(left, 2 * rows)] = ds.astype(BF16)
                dsp[j, :, pl.ds(left + 2 * rows, 2 * rows)] = p.astype(BF16)
            return carry

        lax.fori_loop(0, chunks, combine, 0)
        ds_all = dsp[:, :, pl.ds(left, 2 * rows)].reshape(n * rows, 2 * rows)
        dq = (jnp.dot(kvt[...], ds_all, preferred_element_type=F32) * scale).astype(BF16)
        for u in range(2):
            i = 2 * a + u
            block = dq[:, u * rows : (u + 1) * rows]

            @pl.when(i != head)
            def _():
                dqs[i] = block
                dq_copy(i, head).start()

            @pl.when(i == head)
            def _():
                dqr[head] = block

        if not early:

            def gather(j, carry):
                term = jnp.dot(dsp[j], w_a, preferred_element_type=F32)
                dkv[j] = jnp.where(t == 0, term, dkv[j] + term)
                return carry

            lax.fori_loop(0, n, gather, 0)
        return carry

    lax.fori_loop(0, HEADS // 2, pair_of, 0)

    def key_sums(j):
        if not early:
            return dkv[j]
        return jnp.dot(dsp[j], w[...], preferred_element_type=F32)

    def rd_copy(e, t):
        return remote(
            rds.at[e - 1, t],
            rdr.at[e - 1, t],
            rd_ss.at[e - 1, t],
            rd_rs.at[e - 1, t],
            head * parts + sibling(e),
        )

    for e in range(1, parts):

        def for_sibling(t, carry, e=e):
            rds[e - 1, t] = key_sums(t * parts + sibling(e))
            rd_copy(e, t).start()
            return carry

        lax.fori_loop(0, HEADS, for_sibling, 0)

    def out_copy(t, i):
        return remote(
            outs.at[t], outr.at[head], out_ss.at[t], out_rs.at[t], i * parts + part
        )

    def for_owner(t, carry):
        i = lax.rem(head + t + 1, HEADS)
        total = key_sums(i * parts + part)
        for e in range(1, parts):
            rd_copy(e, i).wait_recv()
            total = total + rdr[e - 1, i]

        @pl.when(t < HEADS - 1)
        def _():
            outs[t] = total.astype(BF16)
            out_copy(t, i).start()

        @pl.when(t == HEADS - 1)
        def _():
            outr[head] = total.astype(BF16)

        return carry

    lax.fori_loop(0, HEADS, for_owner, 0)

    for d in range(1, HEADS):
        dq_copy(peer(d), peer(d)).wait_recv()
    turned_dq = dqr[...].astype(F32).reshape(HEADS * HD, rows).T
    dq_ref[...] = turned_dq.astype(BF16)
    for copy in cv_copies:
        copy.wait_recv()
    conv = cvo[...] + cvr[0].astype(F32) + cvr[1].astype(F32)
    for t in range(HEADS - 1):
        out_copy(t, 0).wait_recv()
    tiles = [outr[h].astype(F32) for h in range(HEADS)]
    dk_ref[...] = jnp.concatenate([tile[:, :HD] for tile in tiles], axis=1).astype(BF16)
    dv_ref[...] = (jnp.concatenate([tile[:, HD:] for tile in tiles], axis=1) + conv).astype(BF16)

    for copy in kv_copies + qg_copies + sm_copies + cv_copies + forwards:
        copy.wait_send()
    for t in range(HEADS - 1):
        dq_copy(peer(t + 1), 0).wait_send()
        out_copy(t, 0).wait_send()
    for e in range(1, parts):
        for t in range(HEADS):
            rd_copy(e, t).wait_send()


def body(queries, keys, values, outputs, grad_out, block_mask, neighbours, conv_weight):
    n = lax.axis_size("blk")
    rows, channels = queries.shape
    parts = n // HEADS
    early = n * rows * rows * HEADS * 8 <= 20 * 2**20
    dma = pltpu.SemaphoreType.DMA
    vmem = pl.BlockSpec(memory_space=pltpu.VMEM)
    shape = jax.ShapeDtypeStruct((rows, channels), BF16)
    others = HEADS - 1
    return pl.pallas_call(
        functools.partial(kernel, n, early),
        out_shape=(shape, shape, shape),
        in_specs=[vmem] * 8,
        out_specs=(vmem, vmem, vmem),
        scratch_shapes=[
            pltpu.VMEM((HEADS, rows, LANES), BF16),
            pltpu.VMEM((HEADS, rows, LANES), BF16),
            pltpu.VMEM((HEADS, 8, LANES), F32),
            pltpu.VMEM((n, rows, LANES), BF16),
            pltpu.VMEM((HEADS, rows, LANES), BF16),
            pltpu.VMEM((HEADS, 8, LANES), F32),
            pltpu.VMEM((HD, n * rows), BF16),
            pltpu.VMEM((HEADS * 2 * rows, LANES), BF16),
            pltpu.VMEM((n, HEADS * 2 * rows), F32),
            pltpu.VMEM((HEADS // 2, 8, 2 * rows), F32),
            pltpu.VMEM((HEADS // 2 if early else 1, n, rows, 4 * rows), F32),
            pltpu.VMEM((n, rows, (HEADS * 2 if early else 4) * rows), BF16),
            pltpu.VMEM((8, LANES) if early else (n, rows, LANES), F32),
            pltpu.VMEM((2, rows, channels), BF16),
            pltpu.VMEM((2, rows, channels), BF16),
            pltpu.VMEM((rows, channels), F32),
            pltpu.VMEM((HEADS, HD, rows), BF16),
            pltpu.VMEM((HEADS, HD, rows), BF16),
            pltpu.VMEM((parts - 1, HEADS, rows, LANES), F32),
            pltpu.VMEM((parts - 1, HEADS, rows, LANES), F32),
            pltpu.VMEM((HEADS, rows, LANES), BF16),
            pltpu.VMEM((HEADS, rows, LANES), BF16),
            dma((others,)),
            dma((others,)),
            dma((others,)),
            dma((others,)),
            dma((others,)),
            dma((others,)),
            dma((parts - 1, HEADS)),
            dma((parts - 1, HEADS)),
            dma((2,)),
            dma((2,)),
            dma((HEADS,)),
            dma((HEADS,)),
            dma((parts - 1, HEADS)),
            dma((parts - 1, HEADS)),
            dma((others,)),
            dma((others,)),
            dma((3,)),
        ],
        compiler_params=pltpu.CompilerParams(
            collective_id=0, has_side_effects=True, vmem_limit_bytes=60 * 2**20
        ),
    )(queries, keys, values, outputs, grad_out, block_mask, neighbours.T, conv_weight)


def solution(mesh):
    tokens = P(("group", "blk"), None)
    return jax.shard_map(
        body,
        mesh=mesh,
        in_specs=(tokens,) * 7 + (P(),),
        out_specs=(tokens,) * 3,
        check_vma=False,
    )
```

```python
import functools

import jax
import jax.numpy as jnp
from jax import lax
from jax.experimental import pallas as pl
from jax.experimental.pallas import tpu as pltpu
from jax.sharding import PartitionSpec as P

HEADS = 8
HD = 64
LANES = 128
F32 = jnp.float32
BF16 = jnp.bfloat16
NEG_LARGE = -1e30
NT = (((1,), (1,)), ((), ()))


def kernel(
    n,
    early,
    q_ref,
    k_ref,
    v_ref,
    o_ref,
    g_ref,
    mask_ref,
    nb_ref,
    cw_ref,
    dq_ref,
    out_ref,
    conv_ref,
    kvs,
    qgs,
    sms,
    kv,
    qg,
    sm,
    kvt,
    w,
    add,
    tops,
    sbuf,
    dsp,
    dkv,
    cvs,
    cvr,
    cvo,
    dqs,
    dqr,
    rds,
    rdr,
    outs,
    outr,
    kv_ss,
    kv_rs,
    qg_ss,
    qg_rs,
    sm_ss,
    sm_rs,
    fw_ss,
    fw_rs,
    cv_ss,
    cv_rs,
    dq_ss,
    dq_rs,
    rd_ss,
    rd_rs,
    out_ss,
    out_rs,
    lc_s,
):
    parts = n // HEADS
    rows = q_ref.shape[0]
    faces = nb_ref.shape[0]
    scale = HD**-0.5
    me = lax.axis_index("blk")
    head = me // parts
    part = me % parts

    def peer(d):
        return lax.rem(head + d, HEADS)

    def sibling(e):
        return lax.rem(part + e, parts)

    def at(index):
        return {"blk": index}

    above, below = lax.rem(me + n - 1, n), lax.rem(me + 1, n)

    barrier = pltpu.get_barrier_semaphore()
    partners = [peer(d) * parts + part for d in range(1, HEADS)]
    partners += [head * parts + sibling(e) for e in range(1, parts)]
    partners += [above, below]
    for other in partners:
        pl.semaphore_signal(barrier, inc=1, device_id=at(other), device_id_type=pl.DeviceIdType.MESH)

    def remote(src, dst, ss, rs, index):
        return pltpu.make_async_remote_copy(
            src_ref=src,
            dst_ref=dst,
            send_sem=ss,
            recv_sem=rs,
            device_id=at(index),
            device_id_type=pl.DeviceIdType.MESH,
        )

    for h in range(HEADS):
        cols = slice(h * HD, (h + 1) * HD)
        scaled = (q_ref[:, cols].astype(F32) * scale).astype(BF16)
        qgs[h] = jnp.concatenate([scaled, g_ref[:, cols]], axis=1)
    sms[...] = jnp.zeros_like(sms)
    for h in range(HEADS):
        cols = slice(h * HD, (h + 1) * HD)
        kvs[h] = jnp.concatenate([k_ref[:, cols], v_ref[:, cols]], axis=1)
    grads = g_ref[...].astype(F32)
    product = grads * o_ref[...].astype(F32)
    channels = product.shape[1]
    pick = (
        lax.broadcasted_iota(jnp.int32, (HEADS, channels), 1) // HD
        == lax.broadcasted_iota(jnp.int32, (HEADS, channels), 0)
    ).astype(F32)
    delta = lax.dot_general(
        pick, product, NT, precision=lax.Precision.HIGHEST, preferred_element_type=F32
    )
    mask_row = jnp.concatenate(
        [mask_ref[...].astype(F32), jnp.zeros((1, LANES - n), F32)], axis=1
    )
    for h in range(HEADS):
        sms[h, 0:1, :] = delta[h : h + 1, :]
        sms[h, 1:2, :] = mask_row

    pl.semaphore_wait(barrier, len(partners))

    def exchange(buffer, target, ss, rs):
        copies = [
            remote(buffer.at[peer(d)], target, ss.at[d - 1], rs.at[d - 1], peer(d) * parts + part)
            for d in range(1, HEADS)
        ]
        for copy in copies:
            copy.start()
        return copies

    own = [
        pltpu.make_async_copy(kvs.at[head], kv.at[me], lc_s.at[0]),
        pltpu.make_async_copy(qgs.at[head], qg.at[head], lc_s.at[1]),
        pltpu.make_async_copy(sms.at[head], sm.at[head], lc_s.at[2]),
    ]
    for copy in own:
        copy.start()
    sm_copies = exchange(sms, sm.at[head], sm_ss, sm_rs)
    qg_copies = exchange(qgs, qg.at[head], qg_ss, qg_rs)
    kv_copies = exchange(kvs, kv.at[me], kv_ss, kv_rs)

    hits, terms = [], []
    for f in range(faces):
        line = nb_ref[f : f + 1, :]
        where_to = jnp.where(line >= 0, line - me * rows + rows, -1)
        slots = lax.broadcasted_iota(jnp.int32, (3 * rows, rows), 0)
        hits.append((slots == where_to).astype(F32).astype(BF16))
        terms.append(grads * cw_ref[f : f + 1, :])
    hit = jnp.concatenate(hits, axis=1)
    term = jnp.concatenate(terms, axis=0)
    high = term.astype(BF16)
    low = (term - high.astype(F32)).astype(BF16)
    for b in range(3):
        block = hit[b * rows : (b + 1) * rows]
        spread = jnp.dot(block, high, preferred_element_type=F32) + jnp.dot(
            block, low, preferred_element_type=F32
        )
        if b == 1:
            cvo[...] = spread
        else:
            cvs[b // 2] = spread.astype(BF16)
    cv_copies = [
        remote(cvs.at[0], cvr.at[0], cv_ss.at[0], cv_rs.at[0], above),
        remote(cvs.at[1], cvr.at[1], cv_ss.at[1], cv_rs.at[1], below),
    ]

    pair = 4 * rows
    for copy in own:
        copy.wait()
    for copy in qg_copies + sm_copies:
        copy.wait_recv()
    first_half = lax.broadcasted_iota(jnp.int32, (rows, LANES), 1) < HD
    eye = lax.broadcasted_iota(jnp.int32, (n, LANES), 0) == lax.broadcasted_iota(
        jnp.int32, (n, LANES), 1
    )
    for i in range(HEADS):
        tile = qg[i].astype(F32)
        at_q = i // 2 * pair + i % 2 * rows
        at_g = at_q + 2 * rows
        w[at_q : at_q + rows, :] = jnp.where(first_half, tile, 0.0).astype(BF16)
        w[at_g : at_g + rows, :] = jnp.where(first_half, 0.0, tile).astype(BF16)
        live = jnp.sum(jnp.where(eye, sm[i, 1:2, :], 0.0), axis=1, keepdims=True)
        add[:, at_q : at_q + rows] = jnp.broadcast_to((1.0 - live) * NEG_LARGE, (n, rows))
        add[:, at_g : at_g + rows] = jnp.broadcast_to(-sm[i, 0:1, :], (n, rows))
    tops[...] = jnp.full_like(tops, -jnp.inf)

    def score(js, a, w_a):
        lhs = jnp.concatenate([kv[j] for j in js], axis=0)
        both = lax.dot_general(lhs, w_a, NT, preferred_element_type=F32)
        slot = a if early else 0
        top = tops[a]
        for b, j in enumerate(js):
            tile = both[b * rows : (b + 1) * rows] + add[pl.ds(j, 1), pl.ds(a * pair, pair)]
            sbuf[slot, j] = tile
            s = tile[:, : 2 * rows]
            top = jnp.maximum(top, jnp.max(s.reshape(rows // 8, 8, 2 * rows), axis=0))
        tops[a] = top

    def turn(j):
        tile = kv[j].astype(F32).T
        kvt[:, pl.ds(pl.multiple_of(j * rows, rows), rows)] = tile[:HD].astype(BF16)

    def arrived(js):
        for j in js:
            turn(j)
        if early:
            for a in range(HEADS // 2):
                score(js, a, w[a * pair : (a + 1) * pair, :])

    forwards = []
    waiting = []
    for d in range(HEADS + 1):
        js = []
        ready = waiting
        waiting = []
        if d < HEADS:
            chip = lax.rem(head - d + HEADS, HEADS)
            source = chip * parts + part
            if d:
                kv_copies[d - 1].wait_recv()
            for e in range(1, parts):
                copy = remote(
                    kv.at[source],
                    kv.at[source],
                    fw_ss.at[e - 1, d],
                    fw_rs.at[e - 1, d],
                    head * parts + sibling(e),
                )
                copy.start()
                forwards.append(copy)
                waiting.append((copy, chip * parts + lax.rem(part - e + parts, parts)))
            js.append(source)
        for copy, j in ready:
            copy.wait_recv()
            js.append(j)
        arrived(js)

    for copy in cv_copies:
        copy.start()

    chunk = 2
    chunks = n // chunk

    def dq_copy(i, u):
        return remote(dqs.at[i], dqr.at[head], dq_ss.at[i], dq_rs.at[u], i * parts + part)

    def pair_of(t, carry):
        a = lax.rem(head // 2 + t + 1, HEADS // 2)
        at_a = pl.multiple_of(a * pair, pair)
        w_a = w[pl.ds(at_a, pair), :]
        slot = a if early else 0
        left = at_a if early else 0
        if not early:

            def scores(c, carry):
                score([c * chunk + b for b in range(chunk)], a, w_a)
                return carry

            lax.fori_loop(0, chunks, scores, 0)
        top = jnp.max(tops[a], axis=0, keepdims=True)

        def weigh(c, total):
            for b in range(chunk):
                e = jnp.exp(sbuf[slot, c * chunk + b, :, : 2 * rows] - top)
                sbuf[slot, c * chunk + b, :, : 2 * rows] = e
                total = total + jnp.sum(e.reshape(rows // 8, 8, 2 * rows), axis=0)
            return total

        total = lax.fori_loop(0, chunks, weigh, jnp.zeros((8, 2 * rows), F32))
        inverse = 1.0 / jnp.sum(total, axis=0, keepdims=True)

        def combine(c, carry):
            for b in range(chunk):
                j = c * chunk + b
                p = sbuf[slot, j, :, : 2 * rows] * inverse
                ds = p * sbuf[slot, j, :, 2 * rows :]
                dsp[j, :, pl.ds(left, 2 * rows)] = ds.astype(BF16)
                dsp[j, :, pl.ds(left + 2 * rows, 2 * rows)] = p.astype(BF16)
            return carry

        lax.fori_loop(0, chunks, combine, 0)
        ds_all = dsp[:, :, pl.ds(left, 2 * rows)].reshape(n * rows, 2 * rows)
        dq = (jnp.dot(kvt[...], ds_all, preferred_element_type=F32) * scale).astype(BF16)
        for u in range(2):
            i = 2 * a + u
            block = dq[:, u * rows : (u + 1) * rows]

            @pl.when(i != head)
            def _():
                dqs[i] = block
                dq_copy(i, head).start()

            @pl.when(i == head)
            def _():
                dqr[head] = block

        if not early:

            def gather(j, carry):
                term = jnp.dot(dsp[j], w_a, preferred_element_type=F32)
                dkv[j] = jnp.where(t == 0, term, dkv[j] + term)
                return carry

            lax.fori_loop(0, n, gather, 0)
        return carry

    lax.fori_loop(0, HEADS // 2, pair_of, 0)

    def key_sums(j):
        if not early:
            return dkv[j]
        return jnp.dot(dsp[j], w[...], preferred_element_type=F32)

    def rd_copy(e, t):
        return remote(
            rds.at[e - 1, t],
            rdr.at[e - 1, t],
            rd_ss.at[e - 1, t],
            rd_rs.at[e - 1, t],
            head * parts + sibling(e),
        )

    for e in range(1, parts):

        def for_sibling(t, carry, e=e):
            rds[e - 1, t] = key_sums(t * parts + sibling(e))
            rd_copy(e, t).start()
            return carry

        lax.fori_loop(0, HEADS, for_sibling, 0)

    def out_copy(t, i):
        return remote(
            outs.at[t], outr.at[head], out_ss.at[t], out_rs.at[t], i * parts + part
        )

    def for_owner(t, carry):
        i = lax.rem(head + t + 1, HEADS)
        total = key_sums(i * parts + part)
        for e in range(1, parts):
            rd_copy(e, i).wait_recv()
            total = total + rdr[e - 1, i]

        @pl.when(t < HEADS - 1)
        def _():
            outs[t] = total.astype(BF16)
            out_copy(t, i).start()

        @pl.when(t == HEADS - 1)
        def _():
            outr[head] = total.astype(BF16)

        return carry

    lax.fori_loop(0, HEADS, for_owner, 0)

    for d in range(1, HEADS):
        dq_copy(peer(d), peer(d)).wait_recv()
    dq_ref[...] = dqr[...]
    for copy in cv_copies:
        copy.wait_recv()
    conv_ref[...] = cvo[...] + cvr[0].astype(F32) + cvr[1].astype(F32)
    for t in range(HEADS - 1):
        out_copy(t, 0).wait_recv()
    out_ref[...] = outr[...]

    for copy in kv_copies + qg_copies + sm_copies + cv_copies + forwards:
        copy.wait_send()
    for t in range(HEADS - 1):
        dq_copy(peer(t + 1), 0).wait_send()
        out_copy(t, 0).wait_send()
    for e in range(1, parts):
        for t in range(HEADS):
            rd_copy(e, t).wait_send()


def assemble(dq_tiles, out_tiles, conv, dq_ref, dk_ref, dv_ref):
    channels = dq_ref.shape[1]
    turned = dq_tiles[...].astype(F32).reshape(channels, LANES).T
    dq_ref[...] = turned.astype(BF16)
    tiles = [out_tiles[h].astype(F32) for h in range(HEADS)]
    dk_ref[...] = jnp.concatenate([tile[:, :HD] for tile in tiles], axis=1).astype(BF16)
    total = jnp.concatenate([tile[:, HD:] for tile in tiles], axis=1) + conv[...]
    dv_ref[...] = total.astype(BF16)


def body(queries, keys, values, outputs, grad_out, block_mask, neighbours, conv_weight):
    n = lax.axis_size("blk")
    rows, channels = queries.shape
    parts = n // HEADS
    early = n * rows * rows * HEADS * 8 <= 20 * 2**20
    dma = pltpu.SemaphoreType.DMA
    vmem = pl.BlockSpec(memory_space=pltpu.VMEM)
    shape = jax.ShapeDtypeStruct((rows, channels), BF16)
    others = HEADS - 1
    dq, out, conv = pl.pallas_call(
        functools.partial(kernel, n, early),
        out_shape=(
            jax.ShapeDtypeStruct((HEADS, HD, rows), BF16),
            jax.ShapeDtypeStruct((HEADS, rows, LANES), BF16),
            jax.ShapeDtypeStruct((rows, channels), F32),
        ),
        in_specs=[vmem] * 8,
        out_specs=(vmem, vmem, vmem),
        scratch_shapes=[
            pltpu.VMEM((HEADS, rows, LANES), BF16),
            pltpu.VMEM((HEADS, rows, LANES), BF16),
            pltpu.VMEM((HEADS, 8, LANES), F32),
            pltpu.VMEM((n, rows, LANES), BF16),
            pltpu.VMEM((HEADS, rows, LANES), BF16),
            pltpu.VMEM((HEADS, 8, LANES), F32),
            pltpu.VMEM((HD, n * rows), BF16),
            pltpu.VMEM((HEADS * 2 * rows, LANES), BF16),
            pltpu.VMEM((n, HEADS * 2 * rows), F32),
            pltpu.VMEM((HEADS // 2, 8, 2 * rows), F32),
            pltpu.VMEM((HEADS // 2 if early else 1, n, rows, 4 * rows), F32),
            pltpu.VMEM((n, rows, (HEADS * 2 if early else 4) * rows), BF16),
            pltpu.VMEM((8, LANES) if early else (n, rows, LANES), F32),
            pltpu.VMEM((2, rows, channels), BF16),
            pltpu.VMEM((2, rows, channels), BF16),
            pltpu.VMEM((rows, channels), F32),
            pltpu.VMEM((HEADS, HD, rows), BF16),
            pltpu.VMEM((HEADS, HD, rows), BF16),
            pltpu.VMEM((parts - 1, HEADS, rows, LANES), F32),
            pltpu.VMEM((parts - 1, HEADS, rows, LANES), F32),
            pltpu.VMEM((HEADS, rows, LANES), BF16),
            pltpu.VMEM((HEADS, rows, LANES), BF16),
            dma((others,)),
            dma((others,)),
            dma((others,)),
            dma((others,)),
            dma((others,)),
            dma((others,)),
            dma((parts - 1, HEADS)),
            dma((parts - 1, HEADS)),
            dma((2,)),
            dma((2,)),
            dma((HEADS,)),
            dma((HEADS,)),
            dma((parts - 1, HEADS)),
            dma((parts - 1, HEADS)),
            dma((others,)),
            dma((others,)),
            dma((3,)),
        ],
        compiler_params=pltpu.CompilerParams(
            collective_id=0, has_side_effects=True, vmem_limit_bytes=60 * 2**20
        ),
    )(queries, keys, values, outputs, grad_out, block_mask, neighbours.T, conv_weight)
    return pl.pallas_call(
        assemble,
        out_shape=(shape, shape, shape),
        in_specs=[vmem] * 3,
        out_specs=(vmem, vmem, vmem),
    )(dq, out, conv)


def solution(mesh):
    tokens = P(("group", "blk"), None)
    return jax.shard_map(
        body,
        mesh=mesh,
        in_specs=(tokens,) * 7 + (P(),),
        out_specs=(tokens,) * 3,
        check_vma=False,
    )
```
